128 devices in a mesh: qrow: 16 (over x_lo, z, core), kcol: 8 (over y, x_hi).
Axes of the slice: x: 4 (x_hi: 2, x_lo: 2; x = x_hi * 2 + x_lo), y: 4, z: 4, core: 2. Of those that a mesh axis runs over, the one named last changes fastest.
Arguments:
- query_rows: bfloat16 [16384, 512], P(('qrow', 'kcol')), may hold values from -6 to 6
- key_rows: bfloat16 [16384, 512], P(('kcol', 'qrow')), may hold values from -6 to 6
- value_rows: bfloat16 [16384, 512], P(('kcol', 'qrow')), may hold values from -6 to 6
- layer_out: bfloat16 [16384, 512], P(('qrow', 'kcol')), may hold values from -6 to 6
- grad_out: bfloat16 [16384, 512], P(('qrow', 'kcol')), may hold values from -6 to 6
- block_order: int32 [128], replicated, may hold values from 0 to 127, each once
- tile_mask: int32 [128, 128], replicated, may hold values from 0 to 1, as said below
Outputs:
- grad_query: float32 [16384, 512], P(('qrow', 'kcol'))
- grad_key: float32 [16384, 512], P(('kcol', 'qrow'))
- grad_value: float32 [16384, 512], P(('kcol', 'qrow'))
The draws below stay inside these ranges and needn't reach their ends.
Inputs may be any that keep to these rules, and one draw needn't show every extreme that they name: block_order is a permutation of 0 to 127. tile_mask[a, b] is 1 exactly where logical blocks a and b lie in the same document and b <= a, where documents are runs of consecutive logical blocks; the diagonal is 1.
All inputs are finite; a program needn't handle non-finite values.
Results may differ from the reference program's by a relative error of at most 0.0035.
Values may be sent and summed in bfloat16 or wider, within the bound.
No kernel may reach another device: no remote copies, remote signals or barrier semaphores. Data moves between devices by JAX's collectives and lax.ppermute only.
A program may use at most 192 MiB of HBM per device.

```python
import math
import jax
import jax.numpy as jnp
from jax import lax

HD = 128
H = 4
BLOCK = 128
BLOCKS = 128
TOKENS = 16384
HDIM = 512


def draw_query_rows(key, part):
    key = jax.random.fold_in(key, 1)
    base = jnp.clip(jax.random.normal(key, (TOKENS, HDIM), jnp.float32), -4.5, 4.5)
    return base.astype(jnp.bfloat16)


def draw_key_rows(key, part):
    key = jax.random.fold_in(key, 2)
    base = jnp.clip(jax.random.normal(key, (TOKENS, HDIM), jnp.float32), -4.5, 4.5)
    return base.astype(jnp.bfloat16)


def draw_tile_mask(key, part):
    key = jax.random.fold_in(key, 5)
    labels = jnp.arange(BLOCKS, dtype=jnp.int32)
    starts = (jax.random.randint(key, (BLOCKS,), 0, 24) == 0) | (labels == 0)
    document = jnp.cumsum(starts.astype(jnp.int32))
    allowed = (document[:, None] == document[None, :]) & (labels[None, :] <= labels[:, None])
    return allowed.astype(jnp.int32)


def block_levels(own_key, dims, shards, least, high):
    level = 1.0
    for dim, parts in shards:
        heights = jax.random.uniform(jax.random.fold_in(jax.random.fold_in(own_key, 6), dim), (parts,), jnp.float32, least / len(shards), high / len(shards))
        level = level * jnp.repeat(jnp.exp(heights), dims[dim] // parts).reshape((-1,) + (1,) * (len(dims) - 1 - dim))
    return level


def scatter_about(rng, dims, deviation, most, split=(), held_as=jnp.bfloat16):
    drawn = jax.random.normal(rng, dims, jnp.float32) * deviation
    if len(split) > 0:
        drawn = block_levels(rng, dims, split, -0.22, 0.18) * drawn
    return jnp.clip(drawn, min=-most, max=most).astype(held_as)


def setup_inputs(seed: int = 0) -> dict:
    key_of = jax.random.split(jax.random.key(seed), 8)
    query_rows = draw_query_rows(jax.random.fold_in(key_of[7], 71), 0)
    key_rows = draw_key_rows(jax.random.fold_in(key_of[7], 71), 0)
    value_rows = scatter_about(key_of[2], (TOKENS, HDIM), 1.0, 6.0, ((0, 128),))
    layer_out = scatter_about(key_of[3], (TOKENS, HDIM), 1.0, 6.0, ((0, 128),))
    grad_out = scatter_about(key_of[4], (TOKENS, HDIM), 1.0, 6.0, ((0, 128),))
    block_order = jax.random.permutation(key_of[5], BLOCKS).astype(jnp.int32)
    tile_mask = draw_tile_mask(jax.random.fold_in(key_of[7], 71), 0)
    return dict(query_rows=query_rows, key_rows=key_rows, value_rows=value_rows, layer_out=layer_out, grad_out=grad_out, block_order=block_order, tile_mask=tile_mask)


def reference(query_rows, key_rows, value_rows, layer_out, grad_out, block_order, tile_mask):
    score_scale = 1.0 / math.sqrt(HD)
    logical = jnp.repeat(block_order.astype(jnp.int32), BLOCK)
    offsets = jnp.arange(TOKENS, dtype=jnp.int32) % BLOCK
    position = logical * BLOCK + offsets
    products = (grad_out.astype(jnp.float32) * layer_out.astype(jnp.float32)).reshape(TOKENS, H, HD)
    delta = lax.optimization_barrier(lax.optimization_barrier(jnp.sum(products, axis=2)).astype(jnp.bfloat16)).astype(jnp.float32)
    key_heads = key_rows.astype(jnp.float32).reshape(TOKENS, H, HD)
    value_heads = value_rows.astype(jnp.float32).reshape(TOKENS, H, HD)
    span = BLOCK * 4
    count = TOKENS // span

    def one_step(carry, step_number):
        key_total, value_total = carry
        start = (step_number * span).astype(jnp.int32)
        query_block = lax.dynamic_slice_in_dim(query_rows, start, span, 0).astype(jnp.float32).reshape(span, H, HD)
        grad_block = lax.dynamic_slice_in_dim(grad_out, start, span, 0).astype(jnp.float32).reshape(span, H, HD)
        delta_block = lax.dynamic_slice_in_dim(delta, start, span, 0)
        logical_block = lax.dynamic_slice_in_dim(logical, start, span, 0)
        position_block = lax.dynamic_slice_in_dim(position, start, span, 0)
        mask_rows = jnp.take(tile_mask, logical_block, axis=0)
        allowed = (jnp.take(mask_rows, logical, axis=1) == 1) & (position[None, :] <= position_block[:, None])
        scores = jnp.einsum('qhd,khd->hqk', query_block, key_heads) * score_scale
        scores = jnp.where(allowed[None], scores, -jnp.inf)
        largest = lax.optimization_barrier(jnp.max(scores, axis=2, keepdims=True))
        log_totals = largest + jnp.log(lax.optimization_barrier(jnp.sum(jnp.exp(scores - largest), axis=2, keepdims=True)))
        probs = jnp.exp(scores - log_totals)
        probs_low = lax.optimization_barrier(probs.astype(jnp.bfloat16)).astype(jnp.float32)
        dprobs = jnp.einsum('qhd,khd->hqk', grad_block, value_heads)
        dscores = probs * (dprobs - jnp.transpose(delta_block)[:, :, None])
        dscores_low = lax.optimization_barrier(dscores.astype(jnp.bfloat16)).astype(jnp.float32)
        grad_query_block = jnp.einsum('hqk,khd->qhd', dscores_low, key_heads) * score_scale
        key_total = key_total + jnp.einsum('hqk,qhd->khd', dscores_low, query_block) * score_scale
        value_total = value_total + jnp.einsum('hqk,qhd->khd', probs_low, grad_block)
        return ((key_total, value_total), grad_query_block.reshape(span, HDIM))
    start_carry = (jnp.zeros((TOKENS, H, HD), jnp.float32), jnp.zeros((TOKENS, H, HD), jnp.float32))
    (key_total, value_total), query_parts = lax.scan(one_step, start_carry, jnp.arange(count, dtype=jnp.int32))
    grad_query = query_parts.reshape(TOKENS, HDIM)
    return (grad_query, key_total.reshape(TOKENS, HDIM), value_total.reshape(TOKENS, HDIM))
```

```python
import functools
import math

import jax
import jax.numpy as jnp
from jax import lax
from jax.experimental import pallas as pl
from jax.experimental.pallas import tpu as pltpu
from jax.sharding import Mesh, PartitionSpec as P

HD = 128
H = 4
B = 128
AXES = ("xl", "z", "c", "y", "xh")
SIZES = (2, 4, 2, 4, 2)
QUERY_AXES = ("xl", "z", "c", "y", "xh")
KEY_AXES = ("y", "xh", "xl", "z", "c")
LOG2E = math.log2(math.e)
SCALE = 1.0 / math.sqrt(HD)
NEG = -1e30
NQ = 16
NK = 32
CH_STATS = 4
CH = 2
PAD = 4
ROWS_Q = 2 * B + 16
ROWS_K = 2 * B
F32 = jnp.float32
BF16 = jnp.bfloat16

RANK, QID, LO, HI, QROW, SID = 0, 32, 48, 64, 80, 96
TABLE = SID + NK + 2 * PAD


def shift(x, axis, size, by):
    return lax.ppermute(x, axis, [(i, (i + by) % size) for i in range(size)])


def shift_x(x, by):
    place = [(v % 2) * 2 + v // 2 for v in range(4)]
    return lax.ppermute(x, ("xl", "xh"), [(place[v], place[(v + by) % 4]) for v in range(4)])


def table_of(block_order, tile_mask):
    xl, z, c, y, xh = (lax.axis_index(name) for name in AXES)
    x = xh * 2 + xl
    step = jnp.arange(4, dtype=jnp.int32)
    from_x = (x - step) % 4
    from_y = (y - step) % 4
    zs = jnp.arange(4, dtype=jnp.int32)
    cores = jnp.stack([c, 1 - c]).astype(jnp.int32)
    key_block = (
        (y * 2 + from_x // 2)[None, :, None] * 16
        + ((from_x % 2)[None, :, None] * 4 + zs[None, None, :]) * 2
        + cores[:, None, None]
    ).reshape(NK)
    query_block = (
        ((xl * 4 + zs[None, :]) * 2 + c) * 8 + from_y[:, None] * 2 + xh
    ).reshape(NQ)
    numbers = jnp.arange(128, dtype=jnp.int32)
    firsts = numbers + 1 - jnp.sum(tile_mask, axis=1)

    def pick(values, index):
        return jnp.sum(jnp.where(index[:, None] == numbers[None, :], values[None, :], 0), axis=1)

    key_ids = pick(block_order, key_block)
    query_ids = pick(block_order, query_block)
    start = pick(firsts, query_ids)
    rank = jnp.sum((key_ids[None, :] < key_ids[:, None]).astype(jnp.int32), axis=1)
    slots = jnp.arange(NK, dtype=jnp.int32)
    sorted_ids = jnp.sum(jnp.where(rank[None, :] == slots[:, None], key_ids[None, :], 0), axis=1)
    low = jnp.sum((key_ids[None, :] < start[:, None]).astype(jnp.int32), axis=1)
    high = jnp.sum((key_ids[None, :] <= query_ids[:, None]).astype(jnp.int32), axis=1)
    row = (from_y[:, None] * 4 + zs[None, :]).reshape(NQ)
    return jnp.concatenate(
        [rank, query_ids, low, high, row, sorted_ids, jnp.full((2 * PAD,), 1000, jnp.int32)]
    ).astype(jnp.int32)


def distance():
    return lax.broadcasted_iota(jnp.int32, (B, B), 0) - lax.broadcasted_iota(jnp.int32, (B, B), 1)


def stats_kernel(table, q0, q1, q2, q3, k0, k1, k2, k3, p0, p1, p2, p3, out, qs, ks, sem):
    for s, piece in enumerate((q0, q1, q2, q3)):
        for z in range(4):
            pltpu.make_async_copy(piece.at[z, pl.ds(0, B)], qs.at[s * 4 + z], sem.at[0]).start()
    for i, piece in enumerate((k0, k1, k2, k3, p0, p1, p2, p3)):
        for z in range(4):
            slot = table[RANK + i * 4 + z]
            pltpu.make_async_copy(piece.at[z, pl.ds(0, B)], ks.at[slot], sem.at[1]).start()
    ks[pl.ds(NK, PAD)] = jnp.zeros((PAD, B, HD), BF16)
    pltpu.make_async_copy(qs, qs, sem.at[0]).wait()
    pltpu.make_async_copy(ks.at[pl.ds(0, NK)], ks.at[pl.ds(0, NK)], sem.at[1]).wait()
    apart = distance()

    def one_query_block(b, carry):
        turned = qs[b].T
        low, high, qid = table[LO + b], table[HI + b], table[QID + b]

        def step(i, state):
            most, total = state
            j = low + i * CH_STATS
            keys = ks[pl.ds(j, CH_STATS)].reshape(CH_STATS * B, HD)
            s = jnp.dot(keys, turned, preferred_element_type=F32) * (SCALE * LOG2E)
            s = jnp.concatenate(
                [
                    jnp.where(apart <= (qid - table[SID + j + t]) * B, s[t * B : (t + 1) * B], NEG)
                    for t in range(CH_STATS)
                ]
            ).reshape(CH_STATS * B // 8, 8, B)
            larger = jnp.maximum(most, jnp.max(s, axis=0))
            total = total * jnp.exp2(most - larger) + jnp.sum(jnp.exp2(s - larger[None]), axis=0)
            return larger, total

        steps = (high - low + CH_STATS - 1) // CH_STATS
        most, total = lax.fori_loop(
            0, steps, step, (jnp.full((8, B), NEG, F32), jnp.zeros((8, B), F32))
        )
        top = jnp.max(most, axis=0, keepdims=True)
        row = table[QROW + b]
        out[pl.ds(row, 1), :] = top
        out[pl.ds(NQ + row, 1), :] = jnp.sum(total * jnp.exp2(most - top), axis=0, keepdims=True)
        return carry

    lax.fori_loop(0, NQ, one_query_block, 0)


def grads_kernel(
    table, logs, q0, q1, q2, q3, k0, k1, k2, k3, p0, p1, p2, p3,
    dq_own, dq_send, dkv_own, dkv_send,
    qs, gs, ds_, ks, vs, kt, dqs, dks, dvs, sem,
):
    for i, piece in enumerate((k0, k1, k2, k3, p0, p1, p2, p3)):
        for z in range(4):
            slot = table[RANK + i * 4 + z]
            pltpu.make_async_copy(piece.at[z, pl.ds(0, B)], ks.at[slot], sem.at[0]).start()
            pltpu.make_async_copy(piece.at[z, pl.ds(B, B)], vs.at[slot], sem.at[1]).start()
    for s, piece in enumerate((q0, q1, q2, q3)):
        for z in range(4):
            n = s * 4 + z
            pltpu.make_async_copy(piece.at[z, pl.ds(0, B)], qs.at[n], sem.at[2]).start()
            pltpu.make_async_copy(piece.at[z, pl.ds(B, B)], gs.at[n], sem.at[3]).start()
            pltpu.make_async_copy(piece.at[z, pl.ds(2 * B, 16)], ds_.at[n], sem.at[4]).start()
    ks[pl.ds(NK, PAD)] = jnp.zeros((PAD, B, HD), BF16)
    vs[pl.ds(NK, PAD)] = jnp.zeros((PAD, B, HD), BF16)
    kt[:, pl.ds(NK * B, PAD * B)] = jnp.zeros((HD, PAD * B), BF16)
    dks[...] = jnp.zeros_like(dks)
    dvs[...] = jnp.zeros_like(dvs)
    pltpu.make_async_copy(ks.at[pl.ds(0, NK)], ks.at[pl.ds(0, NK)], sem.at[0]).wait()
    for j in range(NK):
        kt[:, j * B : (j + 1) * B] = ks[j].T
    pltpu.make_async_copy(vs.at[pl.ds(0, NK)], vs.at[pl.ds(0, NK)], sem.at[1]).wait()
    pltpu.make_async_copy(qs, qs, sem.at[2]).wait()
    pltpu.make_async_copy(gs, gs, sem.at[3]).wait()
    pltpu.make_async_copy(ds_, ds_, sem.at[4]).wait()
    apart = distance()

    def one_query_block(b, carry):
        query, grad = qs[b], gs[b]
        query_turned, grad_turned = query.T, grad.T
        low, high, qid = table[LO + b], table[HI + b], table[QID + b]
        log_row = logs[pl.ds(table[QROW + b], 1), :]
        delta_row = ds_[b][0:1].astype(F32)

        def step(i, dq):
            j = low + i * CH
            keys = ks[pl.ds(j, CH)].reshape(CH * B, HD)
            values = vs[pl.ds(j, CH)].reshape(CH * B, HD)
            s = jnp.dot(keys, query_turned, preferred_element_type=F32)
            p = jnp.exp2(s * (SCALE * LOG2E) - log_row)
            p = jnp.concatenate(
                [
                    jnp.where(apart <= (qid - table[SID + j + t]) * B, p[t * B : (t + 1) * B], 0.0)
                    for t in range(CH)
                ]
            )
            dp = jnp.dot(values, grad_turned, preferred_element_type=F32)
            ds = (p * (dp - delta_row)).astype(BF16)
            dv = jnp.dot(p.astype(BF16), grad, preferred_element_type=F32)
            dk = jnp.dot(ds, query, preferred_element_type=F32)
            dvs[pl.ds(j, CH)] += dv.reshape(CH, B, HD)
            dks[pl.ds(j, CH)] += dk.reshape(CH, B, HD)
            at = pl.multiple_of(j * B, B)
            return dq + jnp.dot(kt[:, pl.ds(at, CH * B)], ds, preferred_element_type=F32)

        steps = (high - low + CH - 1) // CH
        dq = lax.fori_loop(0, steps, step, jnp.zeros((HD, B), F32))
        dqs[b] = dq.T * SCALE
        return carry

    lax.fori_loop(0, NQ, one_query_block, 0)
    for z in range(4):
        dq_own[z] = dqs[z]
        for s in range(1, 4):
            dq_send[s - 1, z] = dqs[s * 4 + z].astype(BF16)
    for s in range(4):
        for z in range(4):
            slot = table[RANK + s * 4 + z]
            dkv_own[s, z, :B] = dks[slot] * SCALE
            dkv_own[s, z, B:] = dvs[slot]
            slot = table[RANK + 16 + s * 4 + z]
            dkv_send[s, z, :B] = (dks[slot] * SCALE).astype(BF16)
            dkv_send[s, z, B:] = dvs[slot].astype(BF16)


ANY = pl.BlockSpec(memory_space=pl.ANY)
SMEM = pl.BlockSpec(memory_space=pltpu.SMEM)
VMEM = pl.BlockSpec(memory_space=pltpu.VMEM)
PARAMS = pltpu.CompilerParams(vmem_limit_bytes=40 * 1024 * 1024)


def stats_call(table, queries, keys):
    return pl.pallas_call(
        stats_kernel,
        out_shape=jax.ShapeDtypeStruct((2 * NQ, B), F32),
        in_specs=[SMEM] + [ANY] * 12,
        out_specs=VMEM,
        scratch_shapes=[
            pltpu.VMEM((NQ, B, HD), BF16),
            pltpu.VMEM((NK + PAD, B, HD), BF16),
            pltpu.SemaphoreType.DMA((2,)),
        ],
        compiler_params=PARAMS,
        name="stats",
    )(table, *queries, *keys)


def grads_call(table, logs, queries, keys):
    return pl.pallas_call(
        grads_kernel,
        out_shape=(
            jax.ShapeDtypeStruct((4, B, HD), F32),
            jax.ShapeDtypeStruct((3, 4, B, HD), BF16),
            jax.ShapeDtypeStruct((4, 4, ROWS_K, HD), F32),
            jax.ShapeDtypeStruct((4, 4, ROWS_K, HD), BF16),
        ),
        in_specs=[SMEM, VMEM] + [ANY] * 12,
        out_specs=(VMEM, VMEM, VMEM, VMEM),
        scratch_shapes=[
            pltpu.VMEM((NQ, B, HD), BF16),
            pltpu.VMEM((NQ, B, HD), BF16),
            pltpu.VMEM((NQ, 16, HD), BF16),
            pltpu.VMEM((NK + PAD, B, HD), BF16),
            pltpu.VMEM((NK + PAD, B, HD), BF16),
            pltpu.VMEM((HD, (NK + PAD) * B), BF16),
            pltpu.VMEM((NQ, B, HD), F32),
            pltpu.VMEM((NK + PAD, B, HD), F32),
            pltpu.VMEM((NK + PAD, B, HD), F32),
            pltpu.SemaphoreType.DMA((5,)),
        ],
        compiler_params=PARAMS,
        name="grads",
    )(table, logs, *queries, *keys)


def heads_first(rows):
    return jnp.transpose(rows.reshape(B, H, HD), (1, 0, 2))


def heads_beside(parts):
    return jnp.transpose(parts, (1, 0, 2)).reshape(B, H * HD)


def body(query_rows, key_rows, value_rows, layer_out, grad_out, block_order, tile_mask):
    table = table_of(block_order, tile_mask)
    products = (grad_out.astype(F32) * layer_out.astype(F32)).reshape(B, H, HD)
    delta = jnp.sum(products, axis=2).astype(BF16)
    delta = jnp.broadcast_to(delta.T[:, None, :], (H, 16, B))
    packed = jnp.concatenate(
        [heads_first(query_rows), heads_first(grad_out), delta, heads_first(key_rows), heads_first(value_rows)],
        axis=1,
    )
    mine = lax.all_to_all(packed, "z", 0, 0)
    query_own, key_own = mine[:, :ROWS_Q], mine[:, ROWS_Q:]
    queries = [query_own] + [shift(query_own, "y", 4, s) for s in range(1, 4)]
    keys = [key_own] + [shift_x(key_own, s) for s in range(1, 4)]
    keys = keys + [shift(piece, "c", 2, 1) for piece in keys]

    stats = stats_call(table, queries, keys)
    every = [stats] + [shift(stats, "y", 4, s) for s in range(1, 4)]
    top = functools.reduce(jnp.maximum, [part[:NQ] for part in every])
    total = sum(part[NQ:] * jnp.exp2(part[:NQ] - top) for part in every)
    logs = top + jnp.log2(total)

    dq_own, dq_send, dkv_own, dkv_send = grads_call(table, logs, queries, keys)
    both = dkv_own + shift(dkv_send, "c", 2, 1).astype(F32)
    dq = dq_own + sum(shift(dq_send[s - 1], "y", 4, -s).astype(F32) for s in range(1, 4))
    dkv = both[0] + sum(shift_x(both[s].astype(BF16), -s).astype(F32) for s in range(1, 4))
    back = lax.all_to_all(jnp.concatenate([dq, dkv], axis=1).astype(BF16), "z", 0, 0)
    back = back.astype(F32)
    return (
        heads_beside(back[:, :B]),
        heads_beside(back[:, B : 2 * B]),
        heads_beside(back[:, 2 * B :]),
    )


def solution(mesh):
    inner = Mesh(mesh.devices.reshape(SIZES), AXES)
    placed = (
        P(QUERY_AXES, None),
        P(KEY_AXES, None),
        P(KEY_AXES, None),
        P(QUERY_AXES, None),
        P(QUERY_AXES, None),
        P(),
        P(),
    )
    return jax.shard_map(
        body,
        mesh=inner,
        in_specs=placed,
        out_specs=(P(QUERY_AXES, None), P(KEY_AXES, None), P(KEY_AXES, None)),
        check_vma=False,
    )
```

```python
import math

import jax
import jax.numpy as jnp
from jax import lax
from jax.experimental import pallas as pl
from jax.experimental.pallas import tpu as pltpu
from jax.sharding import Mesh, PartitionSpec as P

HD = 128
H = 4
B = 128
AXES = ("xl", "z", "c", "y", "xh")
SIZES = (2, 4, 2, 4, 2)
QUERY_AXES = ("xl", "z", "c", "y", "xh")
KEY_AXES = ("y", "xh", "xl", "z", "c")
LOG2E = math.log2(math.e)
SCALE = 1.0 / math.sqrt(HD)
NEG = -1e30
NQ = 32
NK = 16
U_STATS = 8
U = 8
ITEMS = NQ * NK // 2 + 8
ROWS_Q = 2 * B + 16
ROWS_K = 2 * B
F32 = jnp.float32
BF16 = jnp.bfloat16

KID, LO, HI, QROW, ORDER, SID = 0, 16, 32, 48, 80, 120
ROWS_Q = 2 * B + 16
ROWS_K = 2 * B
F32 = jnp.float32
BF16 = jnp.bfloat16
NT = (((1,), (1,)), ((), ()))


def swap_y(x, bits):
    return lax.ppermute(x, "y", [(i, i ^ bits) for i in range(4)])


def swap_x(x, bits):
    place = [(v % 2) * 2 + v // 2 for v in range(4)]
    return lax.ppermute(x, ("xl", "xh"), [(place[v], place[v ^ bits]) for v in range(4)])


def swap_core(x):
    return lax.ppermute(x, "c", [(0, 1), (1, 0)])


def table_of(block_order, tile_mask):
    xl, z, c, y, xh = (lax.axis_index(name) for name in AXES)
    x = xh * 2 + xl
    step = jnp.arange(4, dtype=jnp.int32)
    from_x = x ^ step
    from_y = y ^ step
    zs = jnp.arange(4, dtype=jnp.int32)
    cores = jnp.stack([c, 1 - c]).astype(jnp.int32)
    query_block = (
        (((from_x % 2)[None, :, None] * 4 + zs[None, None, :]) * 2 + cores[:, None, None]) * 8
        + y * 2
        + (from_x // 2)[None, :, None]
    ).reshape(NQ)
    key_block = ((from_y[:, None] * 2 + xh) * 16 + (xl * 4 + zs[None, :]) * 2 + c).reshape(NK)
    numbers = jnp.arange(128, dtype=jnp.int32)
    lasts = numbers - 1 + jnp.sum(tile_mask, axis=0)

    def pick(values, index):
        return jnp.sum(jnp.where(index[:, None] == numbers[None, :], values[None, :], 0), axis=1)

    key_ids = pick(block_order, key_block)
    query_ids = pick(block_order, query_block)
    last = pick(lasts, key_ids)
    rank = jnp.sum((query_ids[None, :] < query_ids[:, None]).astype(jnp.int32), axis=1)
    slots = jnp.arange(NQ, dtype=jnp.int32)
    here = rank[None, :] == slots[:, None]
    sorted_ids = jnp.sum(jnp.where(here, query_ids[None, :], 0), axis=1)
    order = jnp.sum(jnp.where(here, slots[None, :], 0), axis=1)
    low = jnp.sum((query_ids[None, :] < key_ids[:, None]).astype(jnp.int32), axis=1)
    high = jnp.sum((query_ids[None, :] <= last[:, None]).astype(jnp.int32), axis=1)
    row = ((from_x[None, :, None] * 2 + cores[:, None, None]) * 4 + zs[None, None, :]).reshape(NQ)
    return jnp.concatenate(
        [key_ids, low, high, row, order, jnp.zeros((8,), jnp.int32), sorted_ids, jnp.zeros((8,), jnp.int32)]
    ).astype(jnp.int32)


def list_items(table, items, unroll):
    def of_key_block(k, n):
        low, high, kid = table[LO + k], table[HI + k], table[KID + k]
        pairs = jnp.maximum(high - low + 1, 0) // 2

        def one(i, carry):
            j = low + 2 * i
            items[0, n + i] = k
            items[1, n + i] = table[ORDER + j]
            items[2, n + i] = table[ORDER + j + 1]
            items[3, n + i] = (table[SID + j] - kid) * B
            items[4, n + i] = jnp.where(j + 1 < high, (table[SID + j + 1] - kid) * B, -B)
            return carry

        lax.fori_loop(0, pairs, one, 0)
        return n + pairs

    n = lax.fori_loop(0, NK, of_key_block, 0)
    for i in range(unroll):
        for part in range(3):
            items[part, n + i] = 0
        items[3, n + i] = -B
        items[4, n + i] = -B
    return jnp.maximum((n + unroll - 1) // unroll, 1)


def distance():
    return lax.broadcasted_iota(jnp.int32, (B, B), 0) - lax.broadcasted_iota(jnp.int32, (B, B), 1)


def stats_kernel(table, *refs):
    queries, keys = refs[:8], refs[8:12]
    out, qs, ks, most, total, items, sem = refs[12:]
    for s, piece in enumerate(queries):
        pltpu.make_async_copy(piece.at[:, pl.ds(0, B)], qs.at[pl.ds(s * 4, 4)], sem.at[0]).start()
    for s, piece in enumerate(keys):
        pltpu.make_async_copy(piece.at[:, pl.ds(0, B)], ks.at[pl.ds(s * 4, 4)], sem.at[1]).start()
    most[...] = jnp.full_like(most, NEG)
    total[...] = jnp.zeros_like(total)
    steps = list_items(table, items, U_STATS)
    pltpu.make_async_copy(qs, qs, sem.at[0]).wait()
    pltpu.make_async_copy(ks, ks, sem.at[1]).wait()
    apart = distance()

    def one(n):
        query = jnp.concatenate([qs[items[1, n]], qs[items[2, n]]])
        s = lax.dot_general(ks[items[0, n]], query, NT, preferred_element_type=F32)
        found = []
        for t in range(2):
            part = jnp.where(
                apart <= items[3 + t, n], s[:, t * B : (t + 1) * B] * (SCALE * LOG2E), NEG
            ).reshape(B // 8, 8, B)
            largest = jnp.max(part, axis=0)
            found.append((largest, jnp.sum(jnp.exp2(part - largest[None]), axis=0)))
        return found

    def step(i, carry):
        found = [one(i * U_STATS + u) for u in range(U_STATS)]
        for u in range(U_STATS):
            for t, (largest, part) in enumerate(found[u]):
                b = items[1 + t, i * U_STATS + u]
                before = most[b]
                larger = jnp.maximum(before, largest)
                most[b] = larger
                total[b] = total[b] * jnp.exp2(before - larger) + part * jnp.exp2(largest - larger)
        return carry

    lax.fori_loop(0, steps, step, 0)
    for b in range(NQ):
        row = table[QROW + b]
        top = jnp.max(most[b], axis=0, keepdims=True)
        out[pl.ds(row, 1), :] = top
        out[pl.ds(NQ + row, 1), :] = jnp.sum(
            total[b] * jnp.exp2(most[b] - top), axis=0, keepdims=True
        )


def merged(first, second):
    top = jnp.maximum(first[:NQ], second[:NQ])
    total = first[NQ:] * jnp.exp2(first[:NQ] - top) + second[NQ:] * jnp.exp2(second[:NQ] - top)
    return top, total


def grads_kernel(table, s0, s1, *refs):
    queries, keys = refs[:8], refs[8:12]
    dq_own, dq_send, dkv_own, dkv_send = refs[12:16]
    logs, qs, ks, kt, ps, dss, dqs, dks, dvs, items, sem, out_sem = refs[16:]
    for s, piece in enumerate(keys):
        pltpu.make_async_copy(piece, ks.at[pl.ds(s * 4, 4)], sem.at[0]).start()
    for s, piece in enumerate(queries):
        pltpu.make_async_copy(piece, qs.at[pl.ds(s * 4, 4)], sem.at[1]).start()
    dqs[...] = jnp.zeros_like(dqs)
    dks[...] = jnp.zeros_like(dks)
    dvs[...] = jnp.zeros_like(dvs)
    steps = list_items(table, items, U)
    top, total = merged(s0, s1)
    logs[...] = top + jnp.log2(total)
    pltpu.make_async_copy(ks, ks, sem.at[0]).wait()
    for j in range(NK):
        kt[j] = ks[j, :B].T
    pltpu.make_async_copy(qs, qs, sem.at[1]).wait()
    apart = distance()

    def scores_of(n, slot, u):
        k, pair = items[0, n], (items[1, n], items[2, n])
        query = jnp.concatenate([qs[b, :B] for b in pair])
        grad = jnp.concatenate([qs[b, B : 2 * B] for b in pair])
        s = lax.dot_general(ks[k, :B], query, NT, preferred_element_type=F32)
        dp = lax.dot_general(ks[k, B:], grad, NT, preferred_element_type=F32)
        for t, b in enumerate(pair):
            at = slice(t * B, (t + 1) * B)
            p = jnp.exp2(s[:, at] * (SCALE * LOG2E) - logs[pl.ds(table[QROW + b], 1), :])
            p = jnp.where(apart <= items[3 + t, n], p, 0.0)
            delta = qs[b, 2 * B :][0:1].astype(F32)
            ps[slot, u, :, at] = p.astype(BF16)
            dss[slot, u, :, at] = (p * (dp[:, at] - delta)).astype(BF16)

    def sums_of(n, slot, u):
        k, pair = items[0, n], (items[1, n], items[2, n])
        query = jnp.concatenate([qs[b, :B] for b in pair])
        grad = jnp.concatenate([qs[b, B : 2 * B] for b in pair])
        dv = jnp.dot(ps[slot, u], grad, preferred_element_type=F32)
        dk = jnp.dot(dss[slot, u], query, preferred_element_type=F32)
        dq = jnp.dot(kt[k], dss[slot, u], preferred_element_type=F32)
        return k, pair, dq, dk, dv

    def first(i):
        for u in range(U):
            scores_of(i * U + u, i % 2, u)

    def second(i):
        for k, pair, dq, dk, dv in [sums_of(i * U + u, i % 2, u) for u in range(U)]:
            dks[k] += dk
            dvs[k] += dv
            dqs[pair[0]] += dq[:, :B]
            dqs[pair[1]] += dq[:, B:]

    def step(i, carry):
        second(i - 1)
        first(i)
        return carry

    first(0)
    lax.fori_loop(1, steps, step, 0)
    second(steps - 1)
    copies = [
        pltpu.make_async_copy(dqs.at[pl.ds(0, 16)], dq_own, out_sem.at[0]),
        pltpu.make_async_copy(dks.at[pl.ds(0, 4)], dkv_own.at[0], out_sem.at[1]),
        pltpu.make_async_copy(dvs.at[pl.ds(0, 4)], dkv_own.at[1], out_sem.at[2]),
    ]
    for copy in copies:
        copy.start()
    dq_send[...] = dqs[16:].astype(BF16)
    for n in range(3):
        dkv_send[n, 0] = dks[4 * n + 4 : 4 * n + 8].astype(BF16)
        dkv_send[n, 1] = dvs[4 * n + 4 : 4 * n + 8].astype(BF16)
    for copy in copies:
        copy.wait()


ANY = pl.BlockSpec(memory_space=pl.ANY)
HBM = pl.BlockSpec(memory_space=pltpu.HBM)
SMEM = pl.BlockSpec(memory_space=pltpu.SMEM)
VMEM = pl.BlockSpec(memory_space=pltpu.VMEM)
PARAMS = pltpu.CompilerParams(vmem_limit_bytes=40 * 1024 * 1024)


def stats_call(table, queries, keys):
    return pl.pallas_call(
        stats_kernel,
        out_shape=jax.ShapeDtypeStruct((2 * NQ, B), F32),
        in_specs=[SMEM] + [ANY] * 12,
        out_specs=VMEM,
        scratch_shapes=[
            pltpu.VMEM((NQ, B, HD), BF16),
            pltpu.VMEM((NK, B, HD), BF16),
            pltpu.VMEM((NQ, 8, B), F32),
            pltpu.VMEM((NQ, 8, B), F32),
            pltpu.SMEM((5, ITEMS), jnp.int32),
            pltpu.SemaphoreType.DMA((2,)),
        ],
        compiler_params=PARAMS,
        name="stats",
    )(table, *queries, *keys)


def grads_call(table, every, queries, keys):
    return pl.pallas_call(
        grads_kernel,
        out_shape=(
            jax.ShapeDtypeStruct((16, HD, B), F32),
            jax.ShapeDtypeStruct((16, HD, B), BF16),
            jax.ShapeDtypeStruct((2, 4, B, HD), F32),
            jax.ShapeDtypeStruct((3, 2, 4, B, HD), BF16),
        ),
        in_specs=[SMEM] + [VMEM] * 2 + [ANY] * 12,
        out_specs=(ANY, VMEM, ANY, VMEM),
        scratch_shapes=[
            pltpu.VMEM((NQ, B), F32),
            pltpu.VMEM((NQ, ROWS_Q, HD), BF16),
            pltpu.VMEM((NK, ROWS_K, HD), BF16),
            pltpu.VMEM((NK, HD, B), BF16),
            pltpu.VMEM((2, U, B, 2 * B), BF16),
            pltpu.VMEM((2, U, B, 2 * B), BF16),
            pltpu.VMEM((NQ, HD, B), F32),
            pltpu.VMEM((NK, B, HD), F32),
            pltpu.VMEM((NK, B, HD), F32),
            pltpu.SMEM((5, ITEMS), jnp.int32),
            pltpu.SemaphoreType.DMA((2,)),
            pltpu.SemaphoreType.DMA((3,)),
        ],
        compiler_params=PARAMS,
        name="grads",
    )(table, *every, *queries, *keys)


def pack_kernel(query_in, key_in, value_in, out_in, grad_in, packed, query, key, value, out, grad, sem):
    pairs = ((grad_in, grad), (out_in, out), (query_in, query), (key_in, key), (value_in, value))
    copies = [pltpu.make_async_copy(a, b, sem.at[n]) for n, (a, b) in enumerate(pairs)]
    for copy in copies:
        copy.start()
    for copy in copies:
        copy.wait()
    for h in range(H):
        at = slice(h * HD, (h + 1) * HD)
        packed[h, 0:B] = query[:, at]
        packed[h, B : 2 * B] = grad[:, at]
        products = grad[:, at].astype(F32) * out[:, at].astype(F32)
        delta = jnp.sum(products.T, axis=0, keepdims=True)
        packed[h, 2 * B : ROWS_Q] = jnp.broadcast_to(delta, (16, B)).astype(BF16)
        packed[h, ROWS_Q : ROWS_Q + B] = key[:, at]
        packed[h, ROWS_Q + B :] = value[:, at]


def pack_call(*arrays):
    return pl.pallas_call(
        pack_kernel,
        out_shape=jax.ShapeDtypeStruct((H, ROWS_Q + ROWS_K, HD), BF16),
        in_specs=[HBM] * 5,
        out_specs=VMEM,
        scratch_shapes=[pltpu.VMEM((B, H * HD), BF16)] * 5 + [pltpu.SemaphoreType.DMA((5,))],
        compiler_params=pltpu.CompilerParams(vmem_limit_bytes=62 * 1024 * 1024),
        name="pack",
    )(*arrays)


def unpack_kernel(back, dq, dk, dv):
    for h in range(H):
        at = slice(h * HD, (h + 1) * HD)
        dq[:, at] = back[h, 0].astype(F32).T * SCALE
        dk[:, at] = back[h, 1].astype(F32) * SCALE
        dv[:, at] = back[h, 2].astype(F32)


def unpack_call(back):
    return pl.pallas_call(
        unpack_kernel,
        out_shape=(jax.ShapeDtypeStruct((B, H * HD), F32),) * 3,
        in_specs=[VMEM],
        out_specs=(VMEM,) * 3,
        compiler_params=PARAMS,
        name="unpack",
    )(back)


def body(query_rows, key_rows, value_rows, layer_out, grad_out, block_order, tile_mask):
    table = table_of(block_order, tile_mask)
    packed = pack_call(query_rows, key_rows, value_rows, layer_out, grad_out)
    mine = lax.all_to_all(packed, "z", 0, 0)
    query_own, key_own = mine[:, :ROWS_Q], mine[:, ROWS_Q:]
    query_near, key_near = swap_x(query_own, 1), swap_y(key_own, 1)
    query_far, key_far = swap_x(query_own, 3), swap_y(key_own, 3)
    query_last, key_last = swap_x(query_near, 3), swap_y(key_near, 3)
    queries = [query_own, query_near, query_last, query_far]
    queries = queries + [swap_core(piece) for piece in queries]
    keys = [key_own, key_near, key_last, key_far]

    stats = stats_call(table, queries, keys)
    stats = jnp.concatenate(merged(stats, swap_core(stats)))
    stats = jnp.concatenate(merged(stats, swap_x(stats, 1)))
    every = [stats, swap_x(stats, 3)]

    dq_own, dq_send, dkv_own, dkv_send = grads_call(table, every, queries, keys)
    dq_other = swap_core(dq_send)
    dkv_near, dkv_far, dkv_last = (swap_y(dkv_send[n - 1], n) for n in (1, 3, 2))
    both = (dq_own + dq_other.astype(F32)).reshape(4, 4, HD, B)
    dq_near, dq_far, dq_last = (swap_x(both[n].astype(BF16), n) for n in (1, 3, 2))
    dq = both[0] + (dq_near.astype(F32) + dq_far.astype(F32) + dq_last.astype(F32))
    dkv = dkv_own + (dkv_near.astype(F32) + dkv_far.astype(F32) + dkv_last.astype(F32))
    back = jnp.stack([dq, dkv[0], dkv[1]], axis=1).astype(BF16)
    return unpack_call(lax.all_to_all(back, "z", 0, 0))


def solution(mesh):
    inner = Mesh(mesh.devices.reshape(SIZES), AXES)
    placed = (
        P(QUERY_AXES, None),
        P(KEY_AXES, None),
        P(KEY_AXES, None),
        P(QUERY_AXES, None),
        P(QUERY_AXES, None),
        P(),
        P(),
    )
    return jax.shard_map(
        body,
        mesh=inner,
        in_specs=placed,
        out_specs=(P(QUERY_AXES, None), P(KEY_AXES, None), P(KEY_AXES, None)),
        check_vma=False,
    )
```

```python
import math

import jax
import jax.numpy as jnp
from jax import lax
from jax.experimental import pallas as pl
from jax.experimental.pallas import tpu as pltpu
from jax.sharding import Mesh, PartitionSpec as P

HD = 128
H = 4
B = 128
AXES = ("xl", "z", "c", "y", "xh")
SIZES = (2, 4, 2, 4, 2)
QUERY_AXES = ("xl", "z", "c", "y", "xh")
KEY_AXES = ("y", "xh", "xl", "z", "c")
LOG2E = math.log2(math.e)
SCALE = 1.0 / math.sqrt(HD)
NEG = -1e30
NQ = 32
NK = 16
U_STATS = 8
U = 8
ITEMS = NQ * NK // 2 + 8
ROWS_Q = 2 * B + 16
ROWS_K = 2 * B
F32 = jnp.float32
BF16 = jnp.bfloat16

KID, LO, HI, QROW, ORDER, SID = 0, 16, 32, 48, 80, 120
ROWS_Q = 2 * B + 16
ROWS_K = 2 * B
F32 = jnp.float32
BF16 = jnp.bfloat16
NT = (((1,), (1,)), ((), ()))


def swap_y(x, bits):
    return lax.ppermute(x, "y", [(i, i ^ bits) for i in range(4)])


def swap_x(x, bits):
    place = [(v % 2) * 2 + v // 2 for v in range(4)]
    return lax.ppermute(x, ("xl", "xh"), [(place[v], place[v ^ bits]) for v in range(4)])


def swap_z(x, bits):
    return lax.ppermute(x, "z", [(i, i ^ bits) for i in range(4)])


def swap_core(x):
    return lax.ppermute(x, "c", [(0, 1), (1, 0)])


def table_of(block_order, tile_mask):
    xl, z, c, y, xh = (lax.axis_index(name) for name in AXES)
    x = xh * 2 + xl
    step = jnp.arange(4, dtype=jnp.int32)
    from_x = x ^ step
    from_y = y ^ step
    zs = z ^ step
    cores = jnp.stack([c, 1 - c]).astype(jnp.int32)
    query_block = (
        (((from_x % 2)[None, :, None] * 4 + zs[None, None, :]) * 2 + cores[:, None, None]) * 8
        + y * 2
        + (from_x // 2)[None, :, None]
    ).reshape(NQ)
    key_block = ((from_y[:, None] * 2 + xh) * 16 + (xl * 4 + zs[None, :]) * 2 + c).reshape(NK)
    numbers = jnp.arange(128, dtype=jnp.int32)
    lasts = numbers - 1 + jnp.sum(tile_mask, axis=0)

    def pick(values, index):
        return jnp.sum(jnp.where(index[:, None] == numbers[None, :], values[None, :], 0), axis=1)

    key_ids = pick(block_order, key_block)
    query_ids = pick(block_order, query_block)
    last = pick(lasts, key_ids)
    rank = jnp.sum((query_ids[None, :] < query_ids[:, None]).astype(jnp.int32), axis=1)
    slots = jnp.arange(NQ, dtype=jnp.int32)
    here = rank[None, :] == slots[:, None]
    sorted_ids = jnp.sum(jnp.where(here, query_ids[None, :], 0), axis=1)
    order = jnp.sum(jnp.where(here, slots[None, :], 0), axis=1)
    low = jnp.sum((query_ids[None, :] < key_ids[:, None]).astype(jnp.int32), axis=1)
    high = jnp.sum((query_ids[None, :] <= last[:, None]).astype(jnp.int32), axis=1)
    row = ((from_x[None, :, None] * 2 + cores[:, None, None]) * 4 + zs[None, None, :]).reshape(NQ)
    return jnp.concatenate(
        [key_ids, low, high, row, order, jnp.zeros((8,), jnp.int32), sorted_ids, jnp.zeros((8,), jnp.int32)]
    ).astype(jnp.int32)


def list_items(table, items, unroll):
    def of_key_block(k, n):
        low, high, kid = table[LO + k], table[HI + k], table[KID + k]
        pairs = jnp.maximum(high - low + 1, 0) // 2

        def one(i, carry):
            j = low + 2 * i
            items[0, n + i] = k
            items[1, n + i] = table[ORDER + j]
            items[2, n + i] = table[ORDER + j + 1]
            items[3, n + i] = (table[SID + j] - kid) * B
            items[4, n + i] = jnp.where(j + 1 < high, (table[SID + j + 1] - kid) * B, -B)
            return carry

        lax.fori_loop(0, pairs, one, 0)
        return n + pairs

    n = lax.fori_loop(0, NK, of_key_block, 0)
    for i in range(unroll):
        for part in range(3):
            items[part, n + i] = 0
        items[3, n + i] = -B
        items[4, n + i] = -B
    return jnp.maximum((n + unroll - 1) // unroll, 1)


def distance():
    return lax.broadcasted_iota(jnp.int32, (B, B), 0) - lax.broadcasted_iota(jnp.int32, (B, B), 1)


def stats_kernel(table, *refs):
    queries, keys = refs[:8], refs[8:12]
    out, qs, ks, most, total, items, sem = refs[12:]
    for s, piece in enumerate(queries):
        pltpu.make_async_copy(piece.at[:, pl.ds(0, B)], qs.at[pl.ds(s * 4, 4)], sem.at[0]).start()
    for s, piece in enumerate(keys):
        pltpu.make_async_copy(piece.at[:, pl.ds(0, B)], ks.at[pl.ds(s * 4, 4)], sem.at[1]).start()
    most[...] = jnp.full_like(most, NEG)
    total[...] = jnp.zeros_like(total)
    steps = list_items(table, items, U_STATS)
    pltpu.make_async_copy(qs, qs, sem.at[0]).wait()
    pltpu.make_async_copy(ks, ks, sem.at[1]).wait()
    apart = distance()

    def one(n):
        query = jnp.concatenate([qs[items[1, n]], qs[items[2, n]]])
        s = lax.dot_general(ks[items[0, n]], query, NT, preferred_element_type=F32)
        found = []
        for t in range(2):
            part = jnp.where(
                apart <= items[3 + t, n], s[:, t * B : (t + 1) * B] * (SCALE * LOG2E), NEG
            ).reshape(B // 8, 8, B)
            largest = jnp.max(part, axis=0)
            found.append((largest, jnp.sum(jnp.exp2(part - largest[None]), axis=0)))
        return found

    def step(i, carry):
        found = [one(i * U_STATS + u) for u in range(U_STATS)]
        for u in range(U_STATS):
            for t, (largest, part) in enumerate(found[u]):
                b = items[1 + t, i * U_STATS + u]
                before = most[b]
                larger = jnp.maximum(before, largest)
                most[b] = larger
                total[b] = total[b] * jnp.exp2(before - larger) + part * jnp.exp2(largest - larger)
        return carry

    lax.fori_loop(0, steps, step, 0)
    for b in range(NQ):
        row = table[QROW + b]
        top = jnp.max(most[b], axis=0, keepdims=True)
        out[pl.ds(row, 1), :] = top
        out[pl.ds(NQ + row, 1), :] = jnp.sum(
            total[b] * jnp.exp2(most[b] - top), axis=0, keepdims=True
        )


def merged(first, second):
    top = jnp.maximum(first[:NQ], second[:NQ])
    total = first[NQ:] * jnp.exp2(first[:NQ] - top) + second[NQ:] * jnp.exp2(second[:NQ] - top)
    return top, total


def grads_kernel(table, s0, s1, *refs):
    queries, keys = refs[:8], refs[8:12]
    dq_own, dq_send, dkv_own, dkv_send = refs[12:16]
    logs, qs, ks, kt, ps, dss, dqs, dks, dvs, items, sem, out_sem = refs[16:]
    for s, piece in enumerate(keys):
        pltpu.make_async_copy(piece, ks.at[pl.ds(s * 4, 4)], sem.at[0]).start()
    for s, piece in enumerate(queries):
        pltpu.make_async_copy(piece, qs.at[pl.ds(s * 4, 4)], sem.at[1]).start()
    dqs[...] = jnp.zeros_like(dqs)
    dks[...] = jnp.zeros_like(dks)
    dvs[...] = jnp.zeros_like(dvs)
    steps = list_items(table, items, U)
    top, total = merged(s0, s1)
    logs[...] = top + jnp.log2(total)
    pltpu.make_async_copy(ks, ks, sem.at[0]).wait()
    for j in range(NK):
        kt[j] = ks[j, :B].T
    pltpu.make_async_copy(qs, qs, sem.at[1]).wait()
    apart = distance()

    def scores_of(n, slot, u):
        k, pair = items[0, n], (items[1, n], items[2, n])
        query = jnp.concatenate([qs[b, :B] for b in pair])
        grad = jnp.concatenate([qs[b, B : 2 * B] for b in pair])
        s = lax.dot_general(ks[k, :B], query, NT, preferred_element_type=F32)
        dp = lax.dot_general(ks[k, B:], grad, NT, preferred_element_type=F32)
        for t, b in enumerate(pair):
            at = slice(t * B, (t + 1) * B)
            p = jnp.exp2(s[:, at] * (SCALE * LOG2E) - logs[pl.ds(table[QROW + b], 1), :])
            p = jnp.where(apart <= items[3 + t, n], p, 0.0)
            delta = qs[b, 2 * B :][0:1].astype(F32)
            ps[slot, u, :, at] = p.astype(BF16)
            dss[slot, u, :, at] = (p * (dp[:, at] - delta)).astype(BF16)

    def sums_of(n, slot, u):
        k, pair = items[0, n], (items[1, n], items[2, n])
        query = jnp.concatenate([qs[b, :B] for b in pair])
        grad = jnp.concatenate([qs[b, B : 2 * B] for b in pair])
        dv = jnp.dot(ps[slot, u], grad, preferred_element_type=F32)
        dk = jnp.dot(dss[slot, u], query, preferred_element_type=F32)
        dq = jnp.dot(kt[k], dss[slot, u], preferred_element_type=F32)
        return k, pair, dq, dk, dv

    def first(i):
        for u in range(U):
            scores_of(i * U + u, i % 2, u)

    def second(i):
        for k, pair, dq, dk, dv in [sums_of(i * U + u, i % 2, u) for u in range(U)]:
            dks[k] += dk
            dvs[k] += dv
            dqs[pair[0]] += dq[:, :B]
            dqs[pair[1]] += dq[:, B:]

    def step(i, carry):
        second(i - 1)
        first(i)
        return carry

    first(0)
    lax.fori_loop(1, steps, step, 0)
    second(steps - 1)
    copies = [
        pltpu.make_async_copy(dqs.at[pl.ds(0, 16)], dq_own, out_sem.at[0]),
        pltpu.make_async_copy(dks.at[pl.ds(0, 4)], dkv_own.at[0], out_sem.at[1]),
        pltpu.make_async_copy(dvs.at[pl.ds(0, 4)], dkv_own.at[1], out_sem.at[2]),
    ]
    for copy in copies:
        copy.start()
    dq_send[...] = dqs[16:].astype(BF16)
    for n in range(3):
        dkv_send[n, 0] = dks[4 * n + 4 : 4 * n + 8].astype(BF16)
        dkv_send[n, 1] = dvs[4 * n + 4 : 4 * n + 8].astype(BF16)
    for copy in copies:
        copy.wait()


ANY = pl.BlockSpec(memory_space=pl.ANY)
HBM = pl.BlockSpec(memory_space=pltpu.HBM)
SMEM = pl.BlockSpec(memory_space=pltpu.SMEM)
VMEM = pl.BlockSpec(memory_space=pltpu.VMEM)
PARAMS = pltpu.CompilerParams(vmem_limit_bytes=40 * 1024 * 1024)


def stats_call(table, queries, keys):
    return pl.pallas_call(
        stats_kernel,
        out_shape=jax.ShapeDtypeStruct((2 * NQ, B), F32),
        in_specs=[SMEM] + [ANY] * 12,
        out_specs=VMEM,
        scratch_shapes=[
            pltpu.VMEM((NQ, B, HD), BF16),
            pltpu.VMEM((NK, B, HD), BF16),
            pltpu.VMEM((NQ, 8, B), F32),
            pltpu.VMEM((NQ, 8, B), F32),
            pltpu.SMEM((5, ITEMS), jnp.int32),
            pltpu.SemaphoreType.DMA((2,)),
        ],
        compiler_params=PARAMS,
        name="stats",
    )(table, *queries, *keys)


def grads_call(table, every, queries, keys):
    return pl.pallas_call(
        grads_kernel,
        out_shape=(
            jax.ShapeDtypeStruct((16, HD, B), F32),
            jax.ShapeDtypeStruct((16, HD, B), BF16),
            jax.ShapeDtypeStruct((2, 4, B, HD), F32),
            jax.ShapeDtypeStruct((3, 2, 4, B, HD), BF16),
        ),
        in_specs=[SMEM] + [VMEM] * 2 + [ANY] * 12,
        out_specs=(ANY, VMEM, ANY, VMEM),
        scratch_shapes=[
            pltpu.VMEM((NQ, B), F32),
            pltpu.VMEM((NQ, ROWS_Q, HD), BF16),
            pltpu.VMEM((NK, ROWS_K, HD), BF16),
            pltpu.VMEM((NK, HD, B), BF16),
            pltpu.VMEM((2, U, B, 2 * B), BF16),
            pltpu.VMEM((2, U, B, 2 * B), BF16),
            pltpu.VMEM((NQ, HD, B), F32),
            pltpu.VMEM((NK, B, HD), F32),
            pltpu.VMEM((NK, B, HD), F32),
            pltpu.SMEM((5, ITEMS), jnp.int32),
            pltpu.SemaphoreType.DMA((2,)),
            pltpu.SemaphoreType.DMA((3,)),
        ],
        compiler_params=PARAMS,
        name="grads",
    )(table, *every, *queries, *keys)


def pack_kernel(z, query_in, key_in, value_in, out_in, grad_in, p0, p1, p2, p3, query, key, value, out, grad, sem):
    pairs = ((grad_in, grad), (out_in, out), (query_in, query), (key_in, key), (value_in, value))
    copies = [pltpu.make_async_copy(a, b, sem.at[n]) for n, (a, b) in enumerate(pairs)]
    for copy in copies:
        copy.start()
    for copy in copies:
        copy.wait()
    for n, packed in enumerate((p0, p1, p2, p3)):
        at = pl.ds(pl.multiple_of((z[0] ^ n) * HD, HD), HD)
        packed[0:B] = query[:, at]
        packed[B : 2 * B] = grad[:, at]
        products = grad[:, at].astype(F32) * out[:, at].astype(F32)
        delta = jnp.sum(products.T, axis=0, keepdims=True)
        packed[2 * B : ROWS_Q] = jnp.broadcast_to(delta, (16, B)).astype(BF16)
        packed[ROWS_Q : ROWS_Q + B] = key[:, at]
        packed[ROWS_Q + B :] = value[:, at]


def pack_call(*arrays):
    return pl.pallas_call(
        pack_kernel,
        out_shape=(jax.ShapeDtypeStruct((ROWS_Q + ROWS_K, HD), BF16),) * 4,
        in_specs=[SMEM] + [HBM] * 5,
        out_specs=(VMEM,) * 4,
        scratch_shapes=[pltpu.VMEM((B, H * HD), BF16)] * 5 + [pltpu.SemaphoreType.DMA((5,))],
        compiler_params=pltpu.CompilerParams(vmem_limit_bytes=62 * 1024 * 1024),
        name="pack",
    )(*arrays)


def join_kernel(p0, p1, p2, p3, query, key, sem):
    copies = []
    for n, piece in enumerate((p0, p1, p2, p3)):
        copies.append(pltpu.make_async_copy(piece.at[pl.ds(0, ROWS_Q)], query.at[n], sem.at[2 * n]))
        copies.append(
            pltpu.make_async_copy(piece.at[pl.ds(ROWS_Q, ROWS_K)], key.at[n], sem.at[2 * n + 1])
        )
    for copy in copies:
        copy.start()
    for copy in copies:
        copy.wait()


def join_call(pieces):
    return pl.pallas_call(
        join_kernel,
        out_shape=(
            jax.ShapeDtypeStruct((4, ROWS_Q, HD), BF16),
            jax.ShapeDtypeStruct((4, ROWS_K, HD), BF16),
        ),
        in_specs=[ANY] * 4,
        out_specs=(ANY, ANY),
        scratch_shapes=[pltpu.SemaphoreType.DMA((8,))],
        compiler_params=PARAMS,
        name="join",
    )(*pieces)


def unpack_kernel(z, b0, b1, b2, b3, dq, dk, dv):
    for n, back in enumerate((b0, b1, b2, b3)):
        at = pl.ds(pl.multiple_of((z[0] ^ n) * HD, HD), HD)
        dq[:, at] = back[0].astype(F32).T * SCALE
        dk[:, at] = back[1].astype(F32) * SCALE
        dv[:, at] = back[2].astype(F32)


def unpack_call(z, *back):
    return pl.pallas_call(
        unpack_kernel,
        out_shape=(jax.ShapeDtypeStruct((B, H * HD), F32),) * 3,
        in_specs=[SMEM] + [VMEM] * 4,
        out_specs=(VMEM,) * 3,
        compiler_params=PARAMS,
        name="unpack",
    )(z, *back)


def body(query_rows, key_rows, value_rows, layer_out, grad_out, block_order, tile_mask):
    table = table_of(block_order, tile_mask)
    z = lax.axis_index("z").astype(jnp.int32).reshape(1)
    packed = pack_call(z, query_rows, key_rows, value_rows, layer_out, grad_out)
    query_own, key_own = join_call([packed[0]] + [swap_z(packed[n], n) for n in (1, 2, 3)])
    query_near, key_near = swap_x(query_own, 1), swap_y(key_own, 1)
    query_far, key_far = swap_x(query_own, 3), swap_y(key_own, 3)
    query_last, key_last = swap_x(query_near, 3), swap_y(key_near, 3)
    queries = [query_own, query_near, query_last, query_far]
    queries = queries + [swap_core(piece) for piece in queries]
    keys = [key_own, key_near, key_last, key_far]

    stats = stats_call(table, queries, keys)
    stats = jnp.concatenate(merged(stats, swap_core(stats)))
    near, far, last = swap_x(stats, 1), swap_x(stats, 3), swap_x(stats, 2)
    every = [jnp.concatenate(merged(stats, near)), jnp.concatenate(merged(far, last))]

    dq_own, dq_send, dkv_own, dkv_send = grads_call(table, every, queries, keys)
    dq_other = swap_core(dq_send)
    dkv_near, dkv_far, dkv_last = (swap_y(dkv_send[n - 1], n) for n in (1, 3, 2))
    both = (dq_own + dq_other.astype(F32)).reshape(4, 4, HD, B)
    sent = tuple(both[n].astype(BF16) for n in (1, 3, 2))
    sent, dkv_near = lax.optimization_barrier((sent, dkv_near))
    dq_near, dq_far, dq_last = (swap_x(part, n) for part, n in zip(sent, (1, 3, 2)))
    dq = both[0] + (dq_near.astype(F32) + dq_far.astype(F32) + dq_last.astype(F32))
    dkv = dkv_own + (dkv_near.astype(F32) + dkv_far.astype(F32) + dkv_last.astype(F32))
    parts = [jnp.stack([dq[n], dkv[0, n], dkv[1, n]]).astype(BF16) for n in range(4)]
    back = [parts[0]] + [swap_z(parts[n], n) for n in range(1, 4)]
    return unpack_call(z, *back)


def solution(mesh):
    inner = Mesh(mesh.devices.reshape(SIZES), AXES)
    placed = (
        P(QUERY_AXES, None),
        P(KEY_AXES, None),
        P(KEY_AXES, None),
        P(QUERY_AXES, None),
        P(QUERY_AXES, None),
        P(),
        P(),
    )
    return jax.shard_map(
        body,
        mesh=inner,
        in_specs=placed,
        out_specs=(P(QUERY_AXES, None), P(KEY_AXES, None), P(KEY_AXES, None)),
        check_vma=False,
    )
```

```python
import math

import jax
import jax.numpy as jnp
from jax import lax
from jax.experimental import pallas as pl
from jax.experimental.pallas import tpu as pltpu
from jax.sharding import Mesh, PartitionSpec as P

HD = 128
H = 4
B = 128
AXES = ("xl", "z", "c", "y", "xh")
SIZES = (2, 4, 2, 4, 2)
QUERY_AXES = ("xl", "z", "c", "y", "xh")
KEY_AXES = ("y", "xh", "xl", "z", "c")
LOG2E = math.log2(math.e)
SCALE = 1.0 / math.sqrt(HD)
NEG = -1e30
NQ = 32
NK = 16
U_STATS = 16
U = 8
ITEMS = NQ * NK // 2 + 16
ROWS_Q = 2 * B + 16
ROWS_K = 2 * B
F32 = jnp.float32
BF16 = jnp.bfloat16

KID, LO, HI, QROW, ORDER, SID = 0, 16, 32, 48, 80, 120
ROWS_Q = 2 * B + 16
ROWS_K = 2 * B
F32 = jnp.float32
BF16 = jnp.bfloat16
NT = (((1,), (1,)), ((), ()))


def swap_y(x, bits):
    return lax.ppermute(x, "y", [(i, i ^ bits) for i in range(4)])


def swap_x(x, bits):
    place = [(v % 2) * 2 + v // 2 for v in range(4)]
    return lax.ppermute(x, ("xl", "xh"), [(place[v], place[v ^ bits]) for v in range(4)])


def swap_z(x, bits):
    return lax.ppermute(x, "z", [(i, i ^ bits) for i in range(4)])


def swap_core(x):
    return lax.ppermute(x, "c", [(0, 1), (1, 0)])


def table_of(block_order, tile_mask):
    xl, z, c, y, xh = (lax.axis_index(name) for name in AXES)
    x = xh * 2 + xl
    step = jnp.arange(4, dtype=jnp.int32)
    from_x = x ^ step
    from_y = y ^ step
    zs = z ^ step
    cores = jnp.stack([c, 1 - c]).astype(jnp.int32)
    query_block = (
        (((from_x % 2)[None, :, None] * 4 + zs[None, None, :]) * 2 + cores[:, None, None]) * 8
        + y * 2
        + (from_x // 2)[None, :, None]
    ).reshape(NQ)
    key_block = ((from_y[:, None] * 2 + xh) * 16 + (xl * 4 + zs[None, :]) * 2 + c).reshape(NK)
    numbers = jnp.arange(128, dtype=jnp.int32)
    lasts = numbers - 1 + jnp.sum(tile_mask, axis=0)

    def pick(values, index):
        return jnp.sum(jnp.where(index[:, None] == numbers[None, :], values[None, :], 0), axis=1)

    key_ids = pick(block_order, key_block)
    query_ids = pick(block_order, query_block)
    last = pick(lasts, key_ids)
    rank = jnp.sum((query_ids[None, :] < query_ids[:, None]).astype(jnp.int32), axis=1)
    slots = jnp.arange(NQ, dtype=jnp.int32)
    here = rank[None, :] == slots[:, None]
    sorted_ids = jnp.sum(jnp.where(here, query_ids[None, :], 0), axis=1)
    order = jnp.sum(jnp.where(here, slots[None, :], 0), axis=1)
    low = jnp.sum((query_ids[None, :] < key_ids[:, None]).astype(jnp.int32), axis=1)
    high = jnp.sum((query_ids[None, :] <= last[:, None]).astype(jnp.int32), axis=1)
    row = ((from_x[None, :, None] * 2 + cores[:, None, None]) * 4 + zs[None, None, :]).reshape(NQ)
    return jnp.concatenate(
        [key_ids, low, high, row, order, jnp.zeros((8,), jnp.int32), sorted_ids, jnp.zeros((8,), jnp.int32)]
    ).astype(jnp.int32)


def list_items(table, items, unroll):
    def of_key_block(k, n):
        low, high, kid = table[LO + k], table[HI + k], table[KID + k]
        pairs = jnp.maximum(high - low + 1, 0) // 2

        def one(i, carry):
            j = low + 2 * i
            items[0, n + i] = k
            items[1, n + i] = table[ORDER + j]
            items[2, n + i] = table[ORDER + j + 1]
            items[3, n + i] = (table[SID + j] - kid) * B
            items[4, n + i] = jnp.where(j + 1 < high, (table[SID + j + 1] - kid) * B, -B)
            return carry

        lax.fori_loop(0, pairs, one, 0)
        return n + pairs

    n = lax.fori_loop(0, NK, of_key_block, 0)
    for i in range(unroll):
        for part in range(3):
            items[part, n + i] = 0
        items[3, n + i] = -B
        items[4, n + i] = -B
    return jnp.maximum((n + unroll - 1) // unroll, 1)


def distance():
    return lax.broadcasted_iota(jnp.int32, (B, B), 0) - lax.broadcasted_iota(jnp.int32, (B, B), 1)


def stats_kernel(table, *refs):
    queries, keys = refs[:8], refs[8:12]
    out, qs, ks, most, total, items, sem = refs[12:]
    for s, piece in enumerate(queries):
        pltpu.make_async_copy(piece.at[:, pl.ds(0, B)], qs.at[pl.ds(s * 4, 4)], sem.at[0]).start()
    for s, piece in enumerate(keys):
        pltpu.make_async_copy(piece.at[:, pl.ds(0, B)], ks.at[pl.ds(s * 4, 4)], sem.at[1]).start()
    most[...] = jnp.full_like(most, NEG)
    total[...] = jnp.zeros_like(total)
    steps = list_items(table, items, U_STATS)
    pltpu.make_async_copy(qs, qs, sem.at[0]).wait()
    pltpu.make_async_copy(ks, ks, sem.at[1]).wait()
    apart = distance()

    def one(n):
        query = jnp.concatenate([qs[items[1, n]], qs[items[2, n]]])
        s = lax.dot_general(ks[items[0, n]], query, NT, preferred_element_type=F32)
        found = []
        for t in range(2):
            part = jnp.where(
                apart <= items[3 + t, n], s[:, t * B : (t + 1) * B] * (SCALE * LOG2E), NEG
            ).reshape(B // 8, 8, B)
            largest = jnp.max(part, axis=0)
            found.append((largest, jnp.sum(jnp.exp2(part - largest[None]), axis=0)))
        return found

    def step(i, carry):
        found = [one(i * U_STATS + u) for u in range(U_STATS)]
        for u in range(U_STATS):
            for t, (largest, part) in enumerate(found[u]):
                b = items[1 + t, i * U_STATS + u]
                before = most[b]
                larger = jnp.maximum(before, largest)
                most[b] = larger
                total[b] = total[b] * jnp.exp2(before - larger) + part * jnp.exp2(largest - larger)
        return carry

    lax.fori_loop(0, steps, step, 0)
    for b in range(NQ):
        row = table[QROW + b]
        top = jnp.max(most[b], axis=0, keepdims=True)
        out[pl.ds(row, 1), :] = top
        out[pl.ds(NQ + row, 1), :] = jnp.sum(
            total[b] * jnp.exp2(most[b] - top), axis=0, keepdims=True
        )


def merged(first, second):
    top = jnp.maximum(first[:NQ], second[:NQ])
    total = first[NQ:] * jnp.exp2(first[:NQ] - top) + second[NQ:] * jnp.exp2(second[:NQ] - top)
    return top, total


def grads_kernel(table, s0, s1, *refs):
    queries, keys = refs[:8], refs[8:12]
    dq_own, dq_send, dkv_own, dkv_send = refs[12:16]
    logs, qs, ks, kt, ps, dss, dqs, dks, dvs, items, sem, out_sem = refs[16:]
    for s, piece in enumerate(keys):
        pltpu.make_async_copy(piece, ks.at[pl.ds(s * 4, 4)], sem.at[0]).start()
    for s, piece in enumerate(queries):
        pltpu.make_async_copy(piece, qs.at[pl.ds(s * 4, 4)], sem.at[1]).start()
    dqs[...] = jnp.zeros_like(dqs)
    dks[...] = jnp.zeros_like(dks)
    dvs[...] = jnp.zeros_like(dvs)
    steps = list_items(table, items, U)
    top, total = merged(s0, s1)
    logs[...] = top + jnp.log2(total)
    pltpu.make_async_copy(ks, ks, sem.at[0]).wait()
    for j in range(NK):
        kt[j] = ks[j, :B].T
    pltpu.make_async_copy(qs, qs, sem.at[1]).wait()
    apart = distance()

    def scores_of(n, slot, u):
        k, pair = items[0, n], (items[1, n], items[2, n])
        query = jnp.concatenate([qs[b, :B] for b in pair])
        grad = jnp.concatenate([qs[b, B : 2 * B] for b in pair])
        s = lax.dot_general(ks[k, :B], query, NT, preferred_element_type=F32)
        dp = lax.dot_general(ks[k, B:], grad, NT, preferred_element_type=F32)
        for t, b in enumerate(pair):
            at = slice(t * B, (t + 1) * B)
            p = jnp.exp2(s[:, at] * (SCALE * LOG2E) - logs[pl.ds(table[QROW + b], 1), :])
            p = jnp.where(apart <= items[3 + t, n], p, 0.0)
            delta = qs[b, 2 * B :][0:1].astype(F32)
            ps[slot, u, :, at] = p.astype(BF16)
            dss[slot, u, :, at] = (p * (dp[:, at] - delta)).astype(BF16)

    def sums_of(n, slot, u):
        k, pair = items[0, n], (items[1, n], items[2, n])
        query = jnp.concatenate([qs[b, :B] for b in pair])
        grad = jnp.concatenate([qs[b, B : 2 * B] for b in pair])
        dv = jnp.dot(ps[slot, u], grad, preferred_element_type=F32)
        dk = jnp.dot(dss[slot, u], query, preferred_element_type=F32)
        dq = jnp.dot(kt[k], dss[slot, u], preferred_element_type=F32)
        return k, pair, dq, dk, dv

    def first(i):
        for u in range(U):
            scores_of(i * U + u, i % 2, u)

    def second(i):
        for k, pair, dq, dk, dv in [sums_of(i * U + u, i % 2, u) for u in range(U)]:
            dks[k] += dk
            dvs[k] += dv
            dqs[pair[0]] += dq[:, :B]
            dqs[pair[1]] += dq[:, B:]

    def step(i, carry):
        second(i - 1)
        first(i)
        return carry

    first(0)
    lax.fori_loop(1, steps, step, 0)
    second(steps - 1)
    copies = [
        pltpu.make_async_copy(dqs.at[pl.ds(0, 16)], dq_own, out_sem.at[0]),
        pltpu.make_async_copy(dks.at[pl.ds(0, 4)], dkv_own.at[0], out_sem.at[1]),
        pltpu.make_async_copy(dvs.at[pl.ds(0, 4)], dkv_own.at[1], out_sem.at[2]),
    ]
    for copy in copies:
        copy.start()
    dq_send[...] = dqs[16:].astype(BF16)
    for n in range(3):
        dkv_send[n, 0] = dks[4 * n + 4 : 4 * n + 8].astype(BF16)
        dkv_send[n, 1] = dvs[4 * n + 4 : 4 * n + 8].astype(BF16)
    for copy in copies:
        copy.wait()


ANY = pl.BlockSpec(memory_space=pl.ANY)
HBM = pl.BlockSpec(memory_space=pltpu.HBM)
SMEM = pl.BlockSpec(memory_space=pltpu.SMEM)
VMEM = pl.BlockSpec(memory_space=pltpu.VMEM)
PARAMS = pltpu.CompilerParams(vmem_limit_bytes=40 * 1024 * 1024)


def stats_call(table, queries, keys):
    return pl.pallas_call(
        stats_kernel,
        out_shape=jax.ShapeDtypeStruct((2 * NQ, B), F32),
        in_specs=[SMEM] + [ANY] * 12,
        out_specs=VMEM,
        scratch_shapes=[
            pltpu.VMEM((NQ, B, HD), BF16),
            pltpu.VMEM((NK, B, HD), BF16),
            pltpu.VMEM((NQ, 8, B), F32),
            pltpu.VMEM((NQ, 8, B), F32),
            pltpu.SMEM((5, ITEMS), jnp.int32),
            pltpu.SemaphoreType.DMA((2,)),
        ],
        compiler_params=PARAMS,
        name="stats",
    )(table, *queries, *keys)


def grads_call(table, every, queries, keys):
    return pl.pallas_call(
        grads_kernel,
        out_shape=(
            jax.ShapeDtypeStruct((16, HD, B), F32),
            jax.ShapeDtypeStruct((16, HD, B), BF16),
            jax.ShapeDtypeStruct((2, 4, B, HD), F32),
            jax.ShapeDtypeStruct((3, 2, 4, B, HD), BF16),
        ),
        in_specs=[SMEM] + [VMEM] * 2 + [ANY] * 12,
        out_specs=(ANY, VMEM, ANY, VMEM),
        scratch_shapes=[
            pltpu.VMEM((NQ, B), F32),
            pltpu.VMEM((NQ, ROWS_Q, HD), BF16),
            pltpu.VMEM((NK, ROWS_K, HD), BF16),
            pltpu.VMEM((NK, HD, B), BF16),
            pltpu.VMEM((2, U, B, 2 * B), BF16),
            pltpu.VMEM((2, U, B, 2 * B), BF16),
            pltpu.VMEM((NQ, HD, B), F32),
            pltpu.VMEM((NK, B, HD), F32),
            pltpu.VMEM((NK, B, HD), F32),
            pltpu.SMEM((5, ITEMS), jnp.int32),
            pltpu.SemaphoreType.DMA((2,)),
            pltpu.SemaphoreType.DMA((3,)),
        ],
        compiler_params=PARAMS,
        name="grads",
    )(table, *every, *queries, *keys)


def pack_kernel(z, query_in, key_in, value_in, out_in, grad_in, p0, p1, p2, p3, query, key, value, out, grad, sem):
    pairs = ((grad_in, grad), (out_in, out), (query_in, query), (key_in, key), (value_in, value))
    copies = [pltpu.make_async_copy(a, b, sem.at[n]) for n, (a, b) in enumerate(pairs)]
    for copy in copies:
        copy.start()
    for copy in copies:
        copy.wait()
    for n, packed in enumerate((p0, p1, p2, p3)):
        at = pl.ds(pl.multiple_of((z[0] ^ n) * HD, HD), HD)
        packed[0:B] = query[:, at]
        packed[B : 2 * B] = grad[:, at]
        products = grad[:, at].astype(F32) * out[:, at].astype(F32)
        delta = jnp.sum(products.T, axis=0, keepdims=True)
        packed[2 * B : ROWS_Q] = jnp.broadcast_to(delta, (16, B)).astype(BF16)
        packed[ROWS_Q : ROWS_Q + B] = key[:, at]
        packed[ROWS_Q + B :] = value[:, at]


def pack_call(*arrays):
    return pl.pallas_call(
        pack_kernel,
        out_shape=(jax.ShapeDtypeStruct((ROWS_Q + ROWS_K, HD), BF16),) * 4,
        in_specs=[SMEM] + [HBM] * 5,
        out_specs=(VMEM,) * 4,
        scratch_shapes=[pltpu.VMEM((B, H * HD), BF16)] * 5 + [pltpu.SemaphoreType.DMA((5,))],
        compiler_params=pltpu.CompilerParams(vmem_limit_bytes=62 * 1024 * 1024),
        name="pack",
    )(*arrays)


def join_kernel(p0, p1, p2, p3, query, key, sem):
    copies = []
    for n, piece in enumerate((p0, p1, p2, p3)):
        copies.append(pltpu.make_async_copy(piece.at[pl.ds(0, ROWS_Q)], query.at[n], sem.at[2 * n]))
        copies.append(
            pltpu.make_async_copy(piece.at[pl.ds(ROWS_Q, ROWS_K)], key.at[n], sem.at[2 * n + 1])
        )
    for copy in copies:
        copy.start()
    for copy in copies:
        copy.wait()


def join_call(pieces):
    return pl.pallas_call(
        join_kernel,
        out_shape=(
            jax.ShapeDtypeStruct((4, ROWS_Q, HD), BF16),
            jax.ShapeDtypeStruct((4, ROWS_K, HD), BF16),
        ),
        in_specs=[ANY] * 4,
        out_specs=(ANY, ANY),
        scratch_shapes=[pltpu.SemaphoreType.DMA((8,))],
        compiler_params=PARAMS,
        name="join",
    )(*pieces)


def unpack_kernel(z, b0, b1, b2, b3, dq, dk, dv):
    for n, back in enumerate((b0, b1, b2, b3)):
        at = pl.ds(pl.multiple_of((z[0] ^ n) * HD, HD), HD)
        dq[:, at] = back[0].astype(F32).T * SCALE
        dk[:, at] = back[1].astype(F32) * SCALE
        dv[:, at] = back[2].astype(F32)


def unpack_call(z, *back):
    return pl.pallas_call(
        unpack_kernel,
        out_shape=(jax.ShapeDtypeStruct((B, H * HD), F32),) * 3,
        in_specs=[SMEM] + [VMEM] * 4,
        out_specs=(VMEM,) * 3,
        compiler_params=PARAMS,
        name="unpack",
    )(z, *back)


def body(query_rows, key_rows, value_rows, layer_out, grad_out, block_order, tile_mask):
    table = table_of(block_order, tile_mask)
    z = lax.axis_index("z").astype(jnp.int32).reshape(1)
    packed = pack_call(z, query_rows, key_rows, value_rows, layer_out, grad_out)
    p2, p1, p3 = [swap_z(packed[n], n) for n in (2, 1, 3)]
    query_own, key_own = join_call([packed[0], p1, p2, p3])
    query_near, key_near = swap_x(query_own, 1), swap_y(key_own, 1)
    query_far, key_far = swap_x(query_own, 3), swap_y(key_own, 3)
    query_last, key_last = swap_x(query_near, 3), swap_y(key_own, 2)
    queries = [query_own, query_near, query_last, query_far]
    queries = queries + [swap_core(piece) for piece in queries]
    keys = [key_own, key_near, key_last, key_far]

    stats = stats_call(table, queries, keys)
    stats = jnp.concatenate(merged(stats, swap_core(stats)))
    near, far, last = swap_x(stats, 1), swap_x(stats, 3), swap_x(stats, 2)
    every = [jnp.concatenate(merged(stats, near)), jnp.concatenate(merged(far, last))]

    dq_own, dq_send, dkv_own, dkv_send = grads_call(table, every, queries, keys)
    dq_other = swap_core(dq_send)
    dkv_near, dkv_far, dkv_last = (swap_y(dkv_send[n - 1], n) for n in (1, 3, 2))
    both = (dq_own + dq_other.astype(F32)).reshape(4, 4, HD, B)
    sent = tuple(both[n].astype(BF16) for n in (1, 3, 2))
    sent, dkv_near = lax.optimization_barrier((sent, dkv_near))
    dq_near, dq_far, dq_last = (swap_x(part, n) for part, n in zip(sent, (1, 3, 2)))
    dq = both[0] + (dq_near.astype(F32) + dq_far.astype(F32) + dq_last.astype(F32))
    dkv = dkv_own + (dkv_near.astype(F32) + dkv_far.astype(F32) + dkv_last.astype(F32))
    parts = [jnp.stack([dq[n], dkv[0, n], dkv[1, n]]).astype(BF16) for n in range(4)]
    b2, b1, b3 = [swap_z(parts[n], n) for n in (2, 1, 3)]
    back = [parts[0], b1, b2, b3]
    return unpack_call(z, *back)


def solution(mesh):
    inner = Mesh(mesh.devices.reshape(SIZES), AXES)
    placed = (
        P(QUERY_AXES, None),
        P(KEY_AXES, None),
        P(KEY_AXES, None),
        P(QUERY_AXES, None),
        P(QUERY_AXES, None),
        P(),
        P(),
    )
    return jax.shard_map(
        body,
        mesh=inner,
        in_specs=placed,
        out_specs=(P(QUERY_AXES, None), P(KEY_AXES, None), P(KEY_AXES, None)),
        check_vma=False,
    )
```
